32 devices in a mesh: batch: 16 (over z, x, core), tensor: 2 (over y).
Axes of the slice: x: 2, y: 2, z: 4, core: 2. Of those that a mesh axis runs over, the one named last changes fastest.
Arguments:
- residual: float32 [16, 1024, 2048], P('batch', 'tensor'), may hold values from -6 to 6
- segment_ids: int32 [16, 1024], P('batch'), may hold values from 0 to 3, never falling along the last dimension, each value on 1 to 512 neighbouring positions
- norm_gain: float32 [2048], replicated, may hold values from 0.5 to 1.5
- zgate_proj: bfloat16 [2048, 4096], P(None, 'tensor'), may hold values from -0.125 to 0.125
- xin_proj: bfloat16 [2048, 4096], P(None, 'tensor'), may hold values from -0.125 to 0.125
- bc_proj: bfloat16 [2048, 256], replicated, may hold values from -0.125 to 0.125
- dt_proj: bfloat16 [2048, 64], P(None, 'tensor'), may hold values from -0.125 to 0.125
- xconv_weight: float32 [4, 4096], P(None, 'tensor'), may hold values from -3 to 3
- xconv_bias: float32 [4096], P('tensor'), may hold values from -3 to 3
- bcconv_weight: float32 [4, 256], replicated, may hold values from -3 to 3
- bcconv_bias: float32 [256], replicated, may hold values from -3 to 3
- dt_bias: float32 [64], P('tensor'), may hold values from -4 to -1
- decay_log: float32 [64], P('tensor'), may hold values from -4 to 2
- skip_scale: float32 [64], P('tensor'), may hold values from 0.5 to 1.5
- gate_gain: float32 [4096], P('tensor'), may hold values from 0.5 to 1.5
- out_proj: bfloat16 [4096, 2048], P('tensor'), may hold values from -0.09375 to 0.09375
- cotangent: float32 [16, 1024, 2048], P('batch', 'tensor'), may hold values from -6 to 6
Outputs:
- block_output: float32 [16, 1024, 2048], P('batch', 'tensor')
- input_grad: float32 [16, 1024, 2048], P('batch', 'tensor')
- normgain_grad: float32 [2048], replicated
- zproj_grad: float32 [2048, 4096], P(None, 'tensor')
- xproj_grad: float32 [2048, 4096], P(None, 'tensor')
- bcproj_grad: float32 [2048, 256], replicated
- dtproj_grad: float32 [2048, 64], P(None, 'tensor')
- xconv_grad: float32 [4, 4096], P(None, 'tensor')
- xbias_grad: float32 [4096], P('tensor')
- bcconv_grad: float32 [4, 256], replicated
- bcbias_grad: float32 [256], replicated
- dtbias_grad: float32 [64], P('tensor')
- decay_grad: float32 [64], P('tensor')
- skip_grad: float32 [64], P('tensor')
- gategain_grad: float32 [4096], P('tensor')
- outproj_grad: float32 [4096, 2048], P('tensor')
The draws below stay inside these ranges and needn't reach their ends.
Inputs may be any that keep to these rules, and one draw needn't show every extreme that they name: `segment_ids`: along each row the numbers never fall; each document holds 1 to 512 positions and one holds exactly 512.
All inputs are finite; a program needn't handle non-finite values.
Results may differ from the reference program's by a relative error of at most 0.0089.
Values may be sent and summed in bfloat16 or wider, within the bound.
No kernel may reach another device: no remote copies, remote signals or barrier semaphores. Data moves between devices by JAX's collectives and lax.ppermute only.
A program may use at most 320 MiB of HBM per device.

```python
import math
import jax
import jax.numpy as jnp
import numpy as np
from jax import lax

D = 2048
DI = 4096
H = 64
N = 128
KW = 4
GROUP = 256
LEN = 1024
DOCS = 4
MOST = 512
ROWS = 16


def block_levels(stream_key, dims, split, smallest, high):
    level, own = 1.0, jax.random.fold_in(stream_key, 6)
    for position, shards_of in split:
        steps = jnp.exp(jax.random.uniform(jax.random.fold_in(own, position), (shards_of,), jnp.float32, smallest / len(split), high / len(split)))
        level = level * jnp.repeat(steps, dims[position] // shards_of).reshape([-1 if axis == position else 1 for axis in range(len(dims))])
    return level


def length_profile(number_of, total, most, slope):
    loads = [(1 << 20) // math.isqrt(rank ** slope) + 1 for rank in range(2, number_of + 1)]
    rest, counts = total - most - (number_of - 1), [1] * (number_of - 1)
    while rest > 0:
        candidates = [i for i in range(number_of - 1) if counts[i] < most]
        mass, budget = sum([loads[i] for i in candidates]), rest
        for i in candidates:
            extra = min(most - counts[i], max(1, budget * loads[i] // mass), rest)
            counts[i] = counts[i] + extra
            rest = rest - extra
    return np.array([most] + counts)


def uneven(rng, number_of, total, most, slope):
    if number_of == 2:
        one = jax.random.randint(rng, (), max(1, total - most), min(most, total - 1) + 1)
        return jnp.stack([one, total - one])
    lengths = jnp.asarray(length_profile(number_of, total, most, slope), jnp.int32)
    pairs = (number_of - 1) // 2
    source_of, receiver = lengths[1:1 + 2 * pairs:2], lengths[2:2 + 2 * pairs:2]
    room = jnp.minimum(source_of - 1, most - receiver)
    passed = jax.random.randint(jax.random.fold_in(rng, 1), (pairs,), 0, 1 << 20) % (room + 1)
    lengths = lengths.at[1:1 + 2 * pairs:2].set(source_of - passed).at[2:2 + 2 * pairs:2].set(receiver + passed)
    return lengths[jax.random.permutation(jax.random.fold_in(rng, 2), number_of)]


def gaussian(key, shape, width, reach, shards=(), dtype=jnp.bfloat16):
    level = block_levels(key, shape, shards, -0.22, 0.18) if shards else 1.0
    drawn = jax.random.normal(key, shape, jnp.float32) * width * level
    return jnp.minimum(jnp.maximum(drawn, -reach), reach).astype(dtype)


def setup_inputs(seed: int = 0) -> dict:
    key_list = jax.random.split(jax.random.key(seed), 18)
    return {
        "residual": gaussian(key_list[0], (ROWS, LEN, D), 1.0, 6.0, ((0, 16), (1, 2)), jnp.float32),
        "segment_ids": jax.vmap(lambda own: jnp.searchsorted(jnp.cumsum(uneven(own, DOCS, LEN, MOST, 0)), jnp.arange(LEN), side="right"))(jax.random.split(key_list[1], ROWS)).reshape((ROWS, LEN)).astype(jnp.int32),
        "norm_gain": jnp.clip(1.0 + 0.1 * jax.random.normal(key_list[2], (D,), jnp.float32), 0.5, 1.5),
        "zgate_proj": gaussian(key_list[3], (D, DI), D ** -0.5, 0.125, ((1, 2),)),
        "xin_proj": gaussian(key_list[4], (D, DI), D ** -0.5, 0.125, ((1, 2),)),
        "bc_proj": gaussian(key_list[5], (D, 2 * N), D ** -0.5, 0.125),
        "dt_proj": gaussian(key_list[6], (D, H), D ** -0.5, 0.125, ((1, 2),)),
        "xconv_weight": gaussian(key_list[7], (KW, DI), KW ** -0.5, 3.0, ((1, 2),), jnp.float32),
        "xconv_bias": gaussian(key_list[8], (DI,), 0.5, 3.0, ((0, 2),), jnp.float32),
        "bcconv_weight": gaussian(key_list[9], (KW, 2 * N), KW ** -0.5, 3.0, (), jnp.float32),
        "bcconv_bias": gaussian(key_list[10], (2 * N,), 0.5, 3.0, (), jnp.float32),
        "dt_bias": jnp.clip(-4.0 + 3.0 * jax.random.uniform(key_list[11], (H,), jnp.float32) ** block_levels(key_list[11], (H,), ((0, 2),), -0.2, 0.2), -4.0, -1.0),
        "decay_log": jnp.clip(-4.0 + 6.0 * jax.random.uniform(key_list[12], (H,), jnp.float32) ** block_levels(key_list[12], (H,), ((0, 2),), -0.2, 0.2), -4.0, 2.0),
        "skip_scale": jnp.clip(0.5 + 1.0 * jax.random.uniform(key_list[13], (H,), jnp.float32) ** block_levels(key_list[13], (H,), ((0, 2),), -0.2, 0.2), 0.5, 1.5),
        "gate_gain": jnp.clip(1.0 + 0.1 * jax.random.normal(key_list[14], (DI,), jnp.float32), 0.5, 1.5),
        "out_proj": gaussian(key_list[15], (DI, D), DI ** -0.5, 0.09375, ((0, 2),)),
        "cotangent": gaussian(key_list[16], (ROWS, LEN, D), 1.0, 6.0, ((0, 16), (1, 2)), jnp.float32),
    }


EPSILON = 1e-05
HIGHEST = lax.Precision.HIGHEST

@jax.custom_vjp
def low(v):
    return lax.optimization_barrier(v.astype(jnp.bfloat16)).astype(jnp.float32)

@jax.custom_vjp
def low_back(v):
    return v

def low_keep(v):
    return (low(v), None)

def low_pass(kept, grad):
    return (grad,)

def back_keep(v):
    return (v, None)

def back_low(kept, grad):
    return (low(grad),)
low.defvjp(low_keep, low_pass)
low_back.defvjp(back_keep, back_low)

def causal_conv(values, weight, offset, segments):
    summed = offset + weight[0] * values
    for delay_step in range(1, weight.shape[0]):
        shifted = jnp.pad(values, ((0, 0), (delay_step, 0), (0, 0)))[:, :-delay_step]
        earlier = jnp.pad(segments, ((0, 0), (delay_step, 0)), constant_values=-1)[:, :-delay_step]
        summed = summed + weight[delay_step] * jnp.where((earlier == segments)[..., None], shifted, 0.0)
    return summed

def mixer(x_raw, bc_raw, dt_raw, z_raw, xconv_weight, xconv_bias, bcconv_weight, bcconv_bias, dt_bias, decay_log, skip_scale, segments, block_len):
    xconv = jax.nn.silu(causal_conv(x_raw, xconv_weight, xconv_bias, segments))
    bcconv = jax.nn.silu(causal_conv(bc_raw, bcconv_weight, bcconv_bias, segments))
    row_count, length, channels = xconv.shape
    head_count = dt_raw.shape[-1]
    head_size = channels // head_count
    state_size = bcconv.shape[-1] // 2
    block_count = length // block_len
    time_step = jax.nn.softplus(dt_raw + dt_bias)
    logdecay = -jnp.exp(decay_log) * time_step
    heads_view = xconv.reshape(row_count, length, head_count, head_size)
    values = (heads_view * time_step[..., None]).reshape(row_count, block_count, block_len, head_count, head_size)
    keys = bcconv[..., :state_size].reshape(row_count, block_count, block_len, state_size)
    queries = bcconv[..., state_size:].reshape(row_count, block_count, block_len, state_size)
    cumlog = jnp.cumsum(logdecay.reshape(row_count, block_count, block_len, head_count), axis=2)
    blocksegs = segments.reshape(row_count, block_count, block_len)
    positions = jnp.arange(block_len)
    causal = positions[:, None] >= positions[None, :]
    same_doc = (blocksegs[:, :, :, None] == blocksegs[:, :, None, :]) & causal
    scores = jnp.einsum('rctn,rcsn->rcts', queries, keys, precision=HIGHEST)
    log_gap = cumlog[:, :, :, None, :] - cumlog[:, :, None, :, :]
    mixing = jnp.exp(jnp.where(same_doc[..., None], log_gap, -jnp.inf)) * scores[..., None]
    intra = jnp.einsum('rctsh,rcshp->rcthp', mixing, values, precision=HIGHEST)
    last_seg = blocksegs[:, :, -1]
    to_end = jnp.exp(jnp.where((blocksegs == last_seg[:, :, None])[..., None], cumlog[:, :, -1:, :] - cumlog, -jnp.inf))
    weighted = values * to_end[..., None]
    local_state = jnp.einsum('rcshp,rcsn->rchpn', weighted, keys, precision=HIGHEST)
    prev_seg = jnp.concatenate([jnp.full((row_count, 1), -1, jnp.int32), last_seg[:, :-1].astype(jnp.int32)], axis=1)
    decay_gate = jnp.where((last_seg == prev_seg)[..., None], jnp.exp(cumlog[:, :, -1, :]), 0.0)

    def advance(carried, inputs):
        gate_now, state_now = inputs
        return (gate_now[..., None, None] * carried + state_now, carried)
    _, before = lax.scan(advance, jnp.zeros_like(local_state[:, 0]), (jnp.moveaxis(decay_gate, 1, 0), jnp.moveaxis(local_state, 1, 0)))
    before = jnp.moveaxis(before, 0, 1)
    from_start = jnp.where((blocksegs == prev_seg[:, :, None])[..., None], jnp.exp(cumlog), 0.0)
    inter = jnp.einsum('rctn,rchpn->rcthp', queries, before, precision=HIGHEST) * from_start[..., None]
    scanned = (intra + inter).reshape(row_count, length, head_count, head_size) + skip_scale[:, None] * heads_view
    return scanned.reshape(row_count, length, channels) * jax.nn.silu(z_raw)

def matmul(left, right):
    return jnp.dot(left, right, precision=HIGHEST, preferred_element_type=jnp.float32)

def block_row(row_in, row_segments, params):
    norm_gain, zgate_proj, xin_proj, bc_proj, dt_proj, xconv_weight, xconv_bias, bcconv_weight, bcconv_bias, dt_bias, decay_log, skip_scale, gate_gain, out_proj = params
    inv_rms = lax.rsqrt(lax.optimization_barrier(jnp.mean(row_in * row_in, axis=-1, keepdims=True)) + EPSILON)
    normed = low(row_in * inv_rms * norm_gain)
    z_raw = low_back(matmul(normed, zgate_proj))
    x_raw = low_back(matmul(normed, xin_proj))
    bc_raw = low_back(matmul(normed, bc_proj))
    dt_raw = low_back(matmul(normed, dt_proj))
    gated = mixer(x_raw[None], bc_raw[None], dt_raw[None], z_raw[None], xconv_weight, xconv_bias, bcconv_weight, bcconv_bias, dt_bias, decay_log, skip_scale, row_segments[None], GROUP)[0]
    inv_gate = lax.rsqrt(lax.optimization_barrier(jnp.mean(gated * gated, axis=-1, keepdims=True)) + EPSILON)
    normed_gate = low(gated * inv_gate * gate_gain)
    branch = low_back(matmul(normed_gate, out_proj))
    return row_in + branch

def reference(residual, segment_ids, norm_gain, zgate_proj, xin_proj, bc_proj, dt_proj, xconv_weight, xconv_bias, bcconv_weight, bcconv_bias, dt_bias, decay_log, skip_scale, gate_gain, out_proj, cotangent):
    params = tuple((argument.astype(jnp.float32) for argument in (norm_gain, zgate_proj, xin_proj, bc_proj, dt_proj, xconv_weight, xconv_bias, bcconv_weight, bcconv_bias, dt_bias, decay_log, skip_scale, gate_gain, out_proj)))

    def forward(resid_all, weights):

        def one_row(row_pair):
            return jax.checkpoint(block_row)(row_pair[0], row_pair[1], weights)
        return lax.map(one_row, (resid_all, segment_ids))
    block_output, pullback = jax.vjp(forward, residual.astype(jnp.float32), params)
    input_grad, grads = pullback(cotangent.astype(jnp.float32))
    return (block_output, input_grad, grads[0], grads[1], grads[2], grads[3], grads[4], grads[5], grads[6], grads[7], grads[8], grads[9], grads[10], grads[11], grads[12], grads[13])
```

```python
import functools
import jax
import jax.numpy as jnp
from jax import lax
from jax.experimental import pallas as pl
from jax.experimental.pallas import tpu as pltpu
from jax.sharding import Mesh, PartitionSpec as P

EPSILON = 1e-05
BLOCK = 128
LANES = 128
BF = jnp.bfloat16
F32 = jnp.float32
NEG = -1e30
VMEM_LIMIT = 56 * 1024 * 1024


def dot(a, b):
    return jnp.dot(a, b, preferred_element_type=F32)


def dot_nt(a, b):
    return lax.dot_general(a, b, (((1,), (1,)), ((), ())), preferred_element_type=F32)


def dot_tn(a, b):
    return lax.dot_general(a, b, (((0,), (0,)), ((), ())), preferred_element_type=F32)


def dot_exact(a, b):
    return jnp.dot(a, b, precision=lax.Precision.HIGHEST, preferred_element_type=F32)


def iota(shape, dim):
    return lax.broadcasted_iota(jnp.int32, shape, dim)


def sigmoid(v):
    return 1.0 / (1.0 + jnp.exp(-v))


def conv_terms(prev, cur, masks):
    window = jnp.concatenate([prev, cur], axis=0)
    rows = cur.shape[0]
    return [cur] + [masks[k - 1] * window[8 - k : 8 - k + rows] for k in (1, 2, 3)]


def conv_sum(terms, prm):
    total = prm[4:5] + prm[0:1] * terms[0]
    for k in (1, 2, 3):
        total = total + prm[k : k + 1] * terms[k]
    return total


def conv_masks(meta):
    return [meta[:, k : k + 1] for k in (0, 1, 2)]


def split_three(v, heads):
    high = v.astype(BF).astype(F32)
    rest = v - high
    mid = rest.astype(BF).astype(F32)
    low = rest - mid
    return (high + pltpu.roll(mid, heads, 1) + pltpu.roll(low, 2 * heads, 1)).astype(BF)


def prep_kernel(heads, normed, wcat, meta, bcw, aux, raw_o, kq_o, kt_o, qt_o, cum_o, cumt_o, pk_o, halo):
    rows = normed.shape[0]
    state = kt_o.shape[0]

    @pl.when(pl.program_id(0) == 0)
    def _():
        halo[...] = jnp.zeros_like(halo)

    raw = dot(normed[...], wcat[...])
    bc = raw[:, : 2 * state]
    shifted_dt = raw[:, 2 * state :] + aux[0:1]
    raw_o[:, : 2 * state] = bc
    raw_o[:, 2 * state :] = shifted_dt
    m = meta[...]
    conv = conv_sum(conv_terms(halo[...], bc, conv_masks(m)), bcw[...])
    halo[...] = bc[rows - 8 :]
    act = conv * sigmoid(conv)
    kq_o[...] = act.astype(BF)
    kt_o[...] = act[:, :state].T.astype(BF)
    qt_o[...] = act[:, state:].T.astype(BF)
    real = iota((rows, LANES), 1) < heads
    step = jnp.where(
        real, jnp.maximum(shifted_dt, 0.0) + jnp.log1p(jnp.exp(-jnp.abs(shifted_dt))), 0.0
    )
    logdecay = -jnp.exp(aux[1:2]) * step
    tri = (iota((rows, rows), 0) >= iota((rows, rows), 1)).astype(F32)
    cum = dot_exact(tri, logdecay)
    cum_o[...] = cum
    cumt_o[...] = cum.T[: cumt_o.shape[0]]
    start = jnp.where(real, jnp.exp(cum) * m[:, 4:5], 0.0)
    end = jnp.where(real, jnp.exp(cum[rows - 1 :] - cum) * m[:, 5:6], 0.0)
    pk_o[0] = split_three(step, heads)
    pk_o[1] = split_three(start, heads)
    pk_o[2] = split_three(end, heads)


def prep(normed, wcat, meta, bcw, aux, heads, state):
    tokens, width = normed.shape
    hrows = max(8, -(-heads // 8) * 8)
    cols = wcat.shape[1]
    rep = lambda b: (0, 0)
    return pl.pallas_call(
        functools.partial(prep_kernel, heads),
        grid=(tokens // BLOCK,),
        in_specs=[
            pl.BlockSpec((BLOCK, width), lambda b: (b, 0)),
            pl.BlockSpec((width, cols), rep),
            pl.BlockSpec((BLOCK, LANES), lambda b: (b, 0)),
            pl.BlockSpec((8, 2 * state), rep),
            pl.BlockSpec((8, LANES), rep),
        ],
        out_specs=[
            pl.BlockSpec((BLOCK, cols), lambda b: (b, 0)),
            pl.BlockSpec((BLOCK, 2 * state), lambda b: (b, 0)),
            pl.BlockSpec((state, BLOCK), lambda b: (0, b)),
            pl.BlockSpec((state, BLOCK), lambda b: (0, b)),
            pl.BlockSpec((BLOCK, LANES), lambda b: (b, 0)),
            pl.BlockSpec((hrows, BLOCK), lambda b: (0, b)),
            pl.BlockSpec((3, BLOCK, LANES), lambda b: (0, b, 0)),
        ],
        out_shape=[
            jax.ShapeDtypeStruct((tokens, cols), F32),
            jax.ShapeDtypeStruct((tokens, 2 * state), BF),
            jax.ShapeDtypeStruct((state, tokens), BF),
            jax.ShapeDtypeStruct((state, tokens), BF),
            jax.ShapeDtypeStruct((tokens, LANES), F32),
            jax.ShapeDtypeStruct((hrows, tokens), F32),
            jax.ShapeDtypeStruct((3, tokens, LANES), BF),
        ],
        scratch_shapes=[pltpu.VMEM((8, 2 * state), F32)],
        compiler_params=pltpu.CompilerParams(
            dimension_semantics=("arbitrary",), vmem_limit_bytes=VMEM_LIMIT
        ),
        cost_estimate=pl.CostEstimate(
            flops=2 * tokens * width * cols, bytes_accessed=8 << 20, transcendentals=0
        ),
        name="prep",
    )(normed, wcat, meta, bcw, aux)


def head_spread(group, heads, head_size, width):
    r, c = iota((LANES, width), 0), iota((LANES, width), 1)
    head = (group * width + c) // head_size
    hit = (r == head) | (r == head + heads) | (r == head + 2 * heads)
    return jnp.where(hit, 1.0, 0.0).astype(BF)


def head_gather(group, head_size, width):
    c, r = iota((width, LANES), 0), iota((width, LANES), 1)
    return jnp.where(r == (group * width + c) // head_size, 1.0, 0.0).astype(BF)


def reduce_heads(v, gather):
    high = v.astype(BF)
    low = (v - high.astype(F32)).astype(BF)
    return dot(high, gather) + dot(low, gather)


def stack_pair(v, head_size):
    first = iota(v.shape, 1) < head_size
    zero = jnp.zeros_like(v)
    return jnp.concatenate([jnp.where(first, v, zero), jnp.where(first, zero, v)], axis=0)


def fwd_kernel(heads, head_size, state, x, z, meta, segrow, kq, kt, cum, cumt, pk, prm,
               scan_o, before_o, square_o, carried, spread):
    group = pl.program_id(0)
    tokens, width = x.shape
    per_group = width // head_size
    spread[...] = head_spread(group, heads, head_size, width)
    carried[...] = jnp.zeros_like(carried)

    @pl.when(group == 0)
    def _():
        square_o[...] = jnp.zeros_like(square_o)

    p = prm[...]

    @pl.loop(0, tokens // BLOCK)
    def _(b):
        start = pl.multiple_of(b * BLOCK, BLOCK)
        rows = pl.ds(start, BLOCK)
        prev_rows = pl.ds(pl.multiple_of(jnp.maximum(start - 8, 0), 8), 8)
        m = meta[rows]
        masks = conv_masks(m)
        keys, queries = kq[rows, :state], kq[rows, state:]
        scores = dot_nt(queries, keys)
        causal = iota((BLOCK, BLOCK), 0) >= iota((BLOCK, BLOCK), 1)
        shut = jnp.where((m[:, 3:4] == segrow[0:1, rows]) & causal, 0.0, NEG)
        cum_rows = pltpu.roll(cum[rows], lax.rem(LANES - group * per_group, LANES), 1)
        cum_cols = cumt[pl.ds(pl.multiple_of(group * per_group, per_group), per_group), rows]
        step_b = dot(pk[0, rows], spread[...])
        start_b = dot(pk[1, rows], spread[...])
        end_b = dot(pk[2, rows], spread[...])
        old = carried[...]
        before_o[b] = old.astype(BF)
        inter = dot(queries, old.astype(BF)) * start_b
        weighted = []
        square = jnp.zeros((BLOCK, LANES), F32)
        for j in range(width // LANES):
            at = slice(j * LANES, (j + 1) * LANES)
            conv = conv_sum(conv_terms(x[prev_rows, at], x[rows, at], masks), p[:, at])
            xs = conv * sigmoid(conv)
            values = xs * step_b[:, at]
            weighted.append((values * end_b[:, at]).astype(BF))
            pair = stack_pair(values.astype(BF), head_size)
            mixing = []
            for h in range(j * LANES // head_size, (j + 1) * LANES // head_size):
                decay = jnp.exp((cum_rows[:, h : h + 1] - cum_cols[h : h + 1]) + shut)
                mixing.append((decay * scores).astype(BF))
            intra = dot(jnp.concatenate(mixing, axis=1), pair)
            scan = intra + inter[:, at] + p[5:6, at] * xs
            scan_o[rows, at] = scan
            gate = z[rows, at]
            gated = scan * (gate * sigmoid(gate))
            square = square + gated * gated
        square_o[rows] = square_o[rows] + square
        carried[...] = start_b[BLOCK - 1 :] * old + dot(kt[:, rows], jnp.concatenate(weighted, axis=1))


def fwd(x, z, meta, segrow, kq, kt, cum, cumt, pk, prm, heads, head_size, state, width):
    tokens, channels = x.shape
    blocks = tokens // BLOCK
    whole = lambda a: pl.BlockSpec(a.shape, lambda g, n=a.ndim: (0,) * n)
    col = lambda rows: pl.BlockSpec((rows, width), lambda g: (0, g))
    return pl.pallas_call(
        functools.partial(fwd_kernel, heads, head_size, state),
        grid=(channels // width,),
        in_specs=[col(tokens), col(tokens), whole(meta), whole(segrow), whole(kq), whole(kt),
                  whole(cum), whole(cumt), whole(pk), col(8)],
        out_specs=[
            col(tokens),
            pl.BlockSpec((blocks, state, width), lambda g: (0, 0, g)),
            pl.BlockSpec((tokens, LANES), lambda g: (0, 0)),
        ],
        out_shape=[
            jax.ShapeDtypeStruct((tokens, channels), F32),
            jax.ShapeDtypeStruct((blocks, state, channels), BF),
            jax.ShapeDtypeStruct((tokens, LANES), F32),
        ],
        scratch_shapes=[pltpu.VMEM((state, width), F32), pltpu.VMEM((LANES, width), BF)],
        compiler_params=pltpu.CompilerParams(
            dimension_semantics=("arbitrary",), vmem_limit_bytes=VMEM_LIMIT
        ),
        cost_estimate=pl.CostEstimate(
            flops=20 * 1024 * 1024 * 1024, bytes_accessed=32 << 20, transcendentals=0
        ),
        name="scan_forward",
    )(x, z, meta, segrow, kq, kt, cum, cumt, pk, prm)


def bwd_kernel(heads, head_size, state, first_group, x, dy, scan, before, meta, segrow, kq, qt, cum,
               cumt, pk, prm, low_o, dkq_o, dc_o, ds_o, pg_o, carried, spread, gather, later):
    local = pl.program_id(0)
    group = local + first_group
    tokens, width = x.shape
    per_group = width // head_size
    blocks = tokens // BLOCK
    spread[...] = head_spread(group, heads, head_size, width)
    gather[...] = head_gather(group, head_size, width)
    carried[...] = jnp.zeros_like(carried)
    later[...] = jnp.zeros_like(later)
    pg_o[...] = jnp.zeros_like(pg_o)

    @pl.when(local == 0)
    def _():
        dkq_o[...] = jnp.zeros_like(dkq_o)
        dc_o[...] = jnp.zeros_like(dc_o)
        ds_o[...] = jnp.zeros_like(ds_o)

    p = prm[...]

    @pl.loop(0, blocks)
    def _(i):
        b = blocks - 1 - i
        start = pl.multiple_of(b * BLOCK, BLOCK)
        rows = pl.ds(start, BLOCK)
        prev_rows = pl.ds(pl.multiple_of(jnp.maximum(start - 8, 0), 8), 8)
        m = meta[rows]
        masks = conv_masks(m)
        keys, queries = kq[rows, :state], kq[rows, state:]
        scores = dot_nt(keys, queries)
        causal = iota((BLOCK, BLOCK), 0) <= iota((BLOCK, BLOCK), 1)
        shut = jnp.where((m[:, 3:4] == segrow[0:1, rows]) & causal, 0.0, NEG)
        cum_rows = pltpu.roll(cum[rows], lax.rem(LANES - group * per_group, LANES), 1)
        cum_cols = cumt[pl.ds(pl.multiple_of(group * per_group, per_group), per_group), rows]
        step_b = dot(pk[0, rows], spread[...])
        start_b = dot(pk[1, rows], spread[...])
        end_b = dot(pk[2, rows], spread[...])
        ahead = carried[...]
        ahead_low = ahead.astype(BF)
        old = before[b]
        from_state = dot(keys, ahead_low) * end_b
        carry_grad = jnp.sum(old.astype(F32) * ahead, axis=0, keepdims=True) * start_b[BLOCK - 1 :]
        dscores = jnp.zeros((BLOCK, BLOCK), F32)
        weighted, incoming, flow, steps, ends = [], [], [], [], []
        for j in range(width // LANES):
            at = slice(j * LANES, (j + 1) * LANES)
            terms = conv_terms(x[prev_rows, at], x[rows, at], masks)
            conv = conv_sum(terms, p[:, at])
            sig = sigmoid(conv)
            xs = conv * sig
            values = xs * step_b[:, at]
            weighted.append((values * end_b[:, at]).astype(BF))
            values_low = values.astype(BF)
            dy_low = dy[rows, at]
            dy_j = dy_low.astype(F32)
            incoming.append((dy_j * start_b[:, at]).astype(BF))
            outer = dot_nt(stack_pair(values_low, head_size), dy_low)
            mixing = []
            for k, h in enumerate(range(j * LANES // head_size, (j + 1) * LANES // head_size)):
                decay = jnp.exp((cum_cols[h : h + 1] - cum_rows[:, h : h + 1]) + shut)
                mixing.append((decay * scores).astype(BF))
                dscores = dscores + decay * outer[k * BLOCK : (k + 1) * BLOCK]
            dvalues = dot(jnp.concatenate(mixing, axis=1), stack_pair(dy_low, head_size))
            late = from_state[:, at]
            skip = p[5:6, at]
            values_f = values_low.astype(F32)
            total = dvalues + late
            flow.append(dy_j * (scan[rows, at] - skip * xs) - values_f * total)
            ends.append(jnp.sum(values_f * late, axis=0, keepdims=True))
            steps.append(xs * total)
            dxs = step_b[:, at] * total + skip * dy_j
            dconv = dxs * (sig * (1.0 + conv * (1.0 - sig)))
            sums = [jnp.sum(dconv * t, axis=0, keepdims=True) for t in terms]
            sums.append(jnp.sum(dconv, axis=0, keepdims=True))
            sums.append(jnp.sum(dy_j * xs, axis=0, keepdims=True))
            sums.append(jnp.zeros((2, LANES), F32))
            pg_o[:, at] = pg_o[:, at] + jnp.concatenate(sums, axis=0)
            grad = p[0:1, at] * dconv
            for k in (1, 2, 3):
                masked = masks[k - 1] * dconv
                window = jnp.concatenate([masked, later[k - 1, :, at]], axis=0)
                grad = grad + p[k : k + 1, at] * window[k : k + BLOCK]
                later[k - 1, :, at] = masked[:8]
            low_o[rows, at] = grad.astype(BF)
        weighted = jnp.concatenate(weighted, axis=1)
        incoming = jnp.concatenate(incoming, axis=1)
        closing = carry_grad + jnp.concatenate(ends, axis=1)
        flow = jnp.concatenate(flow, axis=1)
        steps = jnp.concatenate(steps, axis=1)
        last = iota((BLOCK, width), 0) == BLOCK - 1
        flow = flow + jnp.where(last, closing, 0.0)
        dc_o[rows] = dc_o[rows] + reduce_heads(flow, gather[...])
        ds_o[rows] = ds_o[rows] + reduce_heads(steps, gather[...])
        dscores_low = dscores.astype(BF)
        dkq_o[rows, :state] = dkq_o[rows, :state] + (
            dot(dscores_low, queries) + dot_nt(weighted, ahead_low)
        )
        dkq_o[rows, state:] = dkq_o[rows, state:] + (
            dot_tn(dscores_low, keys) + dot_nt(incoming, old)
        )
        carried[...] = start_b[BLOCK - 1 :] * ahead + dot(qt[:, rows], incoming)


def bwd(x, dy, scan, before, meta, segrow, kq, qt, cum, cumt, pk, prm, heads, head_size, state, width,
        first_group, groups):
    tokens, channels = x.shape
    blocks = tokens // BLOCK
    whole = lambda a: pl.BlockSpec(a.shape, lambda g, n=a.ndim: (0,) * n)
    col = lambda rows: pl.BlockSpec((rows, width), lambda g: (0, g + first_group))
    out_col = lambda rows: pl.BlockSpec((rows, width), lambda g: (0, g))
    same = lambda g: (0, 0)
    return pl.pallas_call(
        functools.partial(bwd_kernel, heads, head_size, state, first_group),
        grid=(groups,),
        in_specs=[col(tokens), col(tokens), col(tokens),
                  pl.BlockSpec((blocks, state, width), lambda g: (0, 0, g + first_group)),
                  whole(meta), whole(segrow), whole(kq), whole(qt), whole(cum), whole(cumt), whole(pk),
                  col(8)],
        out_specs=[
            out_col(tokens),
            pl.BlockSpec((tokens, 2 * state), same),
            pl.BlockSpec((tokens, LANES), same),
            pl.BlockSpec((tokens, LANES), same),
            out_col(8),
        ],
        out_shape=[
            jax.ShapeDtypeStruct((tokens, groups * width), BF),
            jax.ShapeDtypeStruct((tokens, 2 * state), F32),
            jax.ShapeDtypeStruct((tokens, LANES), F32),
            jax.ShapeDtypeStruct((tokens, LANES), F32),
            jax.ShapeDtypeStruct((8, groups * width), F32),
        ],
        scratch_shapes=[
            pltpu.VMEM((state, width), F32),
            pltpu.VMEM((LANES, width), BF),
            pltpu.VMEM((width, LANES), BF),
            pltpu.VMEM((3, 8, width), F32),
        ],
        compiler_params=pltpu.CompilerParams(
            dimension_semantics=("arbitrary",), vmem_limit_bytes=VMEM_LIMIT
        ),
        cost_estimate=pl.CostEstimate(
            flops=groups * 10 * 1024 * 1024 * 1024, bytes_accessed=groups * (8 << 20), transcendentals=0
        ),
        name="scan_backward",
    )(x, dy, scan, before, meta, segrow, kq, qt, cum, cumt, pk, prm)


def post_kernel(heads, parts, raw, meta, bcw, aux, *refs):
    dkqs, dcs, dss = refs[:parts], refs[parts : 2 * parts], refs[2 * parts : 3 * parts]
    low_o, bg_o, dg_o, later = refs[3 * parts :]
    state2 = bcw.shape[1]
    tokens = raw.shape[0]
    blocks = tokens // BLOCK
    later[...] = jnp.zeros_like(later)
    bg_o[...] = jnp.zeros_like(bg_o)
    dg_o[...] = jnp.zeros_like(dg_o)
    w = bcw[...]
    rate = jnp.exp(aux[1:2])
    real = iota((BLOCK, LANES), 1) < heads

    @pl.loop(0, blocks)
    def _(i):
        b = blocks - 1 - i
        start = pl.multiple_of(b * BLOCK, BLOCK)
        rows = pl.ds(start, BLOCK)
        prev_rows = pl.ds(pl.multiple_of(jnp.maximum(start - 8, 0), 8), 8)
        masks = conv_masks(meta[rows])
        terms = conv_terms(raw[prev_rows, :state2], raw[rows, :state2], masks)
        conv = conv_sum(terms, w)
        sig = sigmoid(conv)
        dact = dkqs[0][rows]
        for r in dkqs[1:]:
            dact = dact + r[rows]
        dconv = dact * (sig * (1.0 + conv * (1.0 - sig)))
        sums = [jnp.sum(dconv * t, axis=0, keepdims=True) for t in terms]
        sums.append(jnp.sum(dconv, axis=0, keepdims=True))
        sums.append(jnp.zeros((3, state2), F32))
        bg_o[...] = bg_o[...] + jnp.concatenate(sums, axis=0)
        grad = w[0:1] * dconv
        for k in (1, 2, 3):
            masked = masks[k - 1] * dconv
            window = jnp.concatenate([masked, later[k - 1]], axis=0)
            grad = grad + w[k : k + 1] * window[k : k + BLOCK]
            later[k - 1] = masked[:8]
        low_o[rows, :state2] = grad.astype(BF)
        flow, direct = dcs[0][rows], dss[0][rows]
        for r in dcs[1:]:
            flow = flow + r[rows]
        for r in dss[1:]:
            direct = direct + r[rows]
        shifted_dt = raw[rows, state2:]
        step = jnp.maximum(shifted_dt, 0.0) + jnp.log1p(jnp.exp(-jnp.abs(shifted_dt)))
        tri = (iota((BLOCK, BLOCK), 0) <= iota((BLOCK, BLOCK), 1)).astype(F32)
        dlog = dot_exact(tri, flow)
        decay_sum = jnp.sum(jnp.where(real, dlog * (-rate * step), 0.0), axis=0, keepdims=True)
        grad_dt = jnp.where(real, (direct - rate * dlog) * sigmoid(shifted_dt), 0.0)
        low_o[rows, state2:] = grad_dt.astype(BF)
        dg_o[...] = dg_o[...] + jnp.concatenate(
            [jnp.sum(grad_dt, axis=0, keepdims=True), decay_sum, jnp.zeros((6, LANES), F32)], axis=0
        )


def post(raw, meta, bcw, aux, dkqs, dcs, dss, heads):
    tokens, cols = raw.shape
    return pl.pallas_call(
        functools.partial(post_kernel, heads, len(dkqs)),
        out_shape=[
            jax.ShapeDtypeStruct((tokens, cols), BF),
            jax.ShapeDtypeStruct((8, bcw.shape[1]), F32),
            jax.ShapeDtypeStruct((8, LANES), F32),
        ],
        scratch_shapes=[pltpu.VMEM((3, 8, bcw.shape[1]), F32)],
        compiler_params=pltpu.CompilerParams(vmem_limit_bytes=VMEM_LIMIT),
        cost_estimate=pl.CostEstimate(flops=1 << 32, bytes_accessed=16 << 20, transcendentals=0),
        name="post",
    )(raw, meta, bcw, aux, *dkqs, *dcs, *dss)


def position_facts(segments):
    row_count, length = segments.shape
    docs = (segments + 1024 * lax.broadcasted_iota(jnp.int32, segments.shape, 0)).reshape(-1)
    tokens = docs.shape[0]
    cols = []
    for k in (1, 2, 3):
        earlier = jnp.concatenate([jnp.full((k,), -1, jnp.int32), docs[:-k]])
        cols.append(earlier == docs)
    tiles = docs.reshape(tokens // BLOCK, BLOCK)
    last = tiles[:, -1:]
    prev = jnp.concatenate([jnp.full((1, 1), -1, jnp.int32), last[:-1]], axis=0)
    cols.append(docs)
    cols.append((tiles == prev).reshape(-1))
    cols.append((tiles == last).reshape(-1))
    lane = lax.broadcasted_iota(jnp.int32, (tokens, LANES), 1)
    meta = jnp.zeros((tokens, LANES), F32)
    for i, c in enumerate(cols):
        meta = jnp.where(lane == i, c.astype(F32)[:, None], meta)
    segrow = jnp.broadcast_to(docs.astype(F32)[None], (8, tokens))
    return meta, segrow


def shards(tensor_count, residual, segment_ids, norm_gain, zgate_proj, xin_proj, bc_proj, dt_proj,
           xconv_weight, xconv_bias, bcconv_weight, bcconv_bias, dt_bias, decay_log, skip_scale,
           gate_gain, out_proj, cotangent):
    row_count, share_len, model_width = residual.shape
    channels, heads = zgate_proj.shape[1], dt_proj.shape[1]
    head_size = channels // heads
    state = bc_proj.shape[1] // 2
    inner = channels * tensor_count
    width = min(512, channels)
    groups = channels // width
    every = ("z", "x", "core")

    inv_rms = lax.rsqrt(jnp.mean(residual * residual, axis=-1, keepdims=True) + EPSILON)
    normed_low = (residual * inv_rms * norm_gain).astype(BF)
    gathered = lax.all_gather(normed_low, "tensor", axis=1, tiled=True)
    length = gathered.shape[1]
    tokens = row_count * length
    normed = gathered.reshape(tokens, model_width)
    cot_low = cotangent.astype(BF)
    cot = lax.all_gather(cot_low, "tensor", axis=1, tiled=True).reshape(tokens, model_width)

    meta, segrow = position_facts(segment_ids)
    wcat = jnp.concatenate([bc_proj, jnp.pad(dt_proj, ((0, 0), (0, LANES - heads)))], axis=1)
    bcw = jnp.concatenate([bcconv_weight, bcconv_bias[None], jnp.zeros((3, 2 * state), F32)], axis=0)
    aux = jnp.pad(jnp.stack([dt_bias, decay_log]), ((0, 6), (0, LANES - heads)))
    prm = jnp.concatenate(
        [xconv_weight, xconv_bias[None], jnp.repeat(skip_scale, head_size)[None],
         jnp.zeros((2, channels), F32)], axis=0)

    z_raw = dot(normed, zgate_proj)
    x_raw = dot(normed, xin_proj)
    raw, kq, kt, qt, cum, cumt, pk = prep(normed, wcat, meta, bcw, aux, heads, state)
    scan, before, square = fwd(
        x_raw, z_raw, meta, segrow, kq, kt, cum, cumt, pk, prm, heads, head_size, state, width)
    grad_normed_gate = dot_nt(cot, out_proj)
    gate_sig = jax.nn.sigmoid(z_raw)
    gate_act = z_raw * gate_sig
    gated = scan * gate_act
    scaled = grad_normed_gate * gate_gain
    stats = lax.psum(
        jnp.stack([jnp.sum(square, axis=-1), jnp.sum(scaled * gated, axis=-1)]), "tensor")
    inv_gate = lax.rsqrt(stats[0] / inner + EPSILON)[:, None]
    pull = inv_gate**3 * (stats[1] / inner)[:, None]
    gate_low = (gated * inv_gate * gate_gain).astype(BF)
    gategain_part = jnp.sum(grad_normed_gate * gated * inv_gate, axis=0)
    grad_gated = inv_gate * scaled - gated * pull
    low_z = (grad_gated * scan * (gate_sig * (1.0 + z_raw * (1.0 - gate_sig)))).astype(BF)
    dy = (grad_gated * gate_act).astype(BF)

    outproj_part = dot_tn(gate_low, cot).astype(BF)
    outproj_grad = lax.psum(outproj_part, every).astype(F32)
    zproj_part = dot_tn(normed, low_z).astype(BF)
    zproj_grad = lax.psum(zproj_part, every).astype(F32)

    partial_out = dot(gate_low, out_proj).astype(BF).reshape(row_count, length, model_width)
    branch = lax.psum_scatter(partial_out, "tensor", scatter_dimension=1, tiled=True)
    block_output = residual + branch.astype(F32)

    low_x, dkq, dc, ds, pg = bwd(
        x_raw, dy, scan, before, meta, segrow, kq, qt, cum, cumt, pk, prm, heads, head_size, state,
        width, 0, groups)
    xproj_part = dot_tn(normed, low_x).astype(BF)
    xproj_grad = lax.psum(xproj_part, every).astype(F32)
    low_small, bg, dg = post(raw, meta, bcw, aux, [dkq], [dc], [ds], heads)
    small_part = dot_tn(low_small, normed)

    grad_part = dot_nt(low_z, zgate_proj) + dot_nt(low_x, xin_proj) + dot_nt(low_small, wcat)
    grad_normed = lax.psum_scatter(
        grad_part.astype(BF).reshape(row_count, length, model_width), "tensor", scatter_dimension=1,
        tiled=True).astype(F32)
    scaled_in = grad_normed * norm_gain
    normgain_part = jnp.sum(grad_normed * residual * inv_rms, axis=(0, 1))
    input_grad = (
        cotangent + inv_rms * scaled_in
        - residual * inv_rms**3 * jnp.mean(scaled_in * residual, axis=-1, keepdims=True))

    skip_part = jnp.sum(pg[5].reshape(heads, head_size), axis=-1)
    bcproj_t, bg, normgain_grad = lax.psum(
        (small_part[: 2 * state], bg, normgain_part), every + ("tensor",))
    dtproj_t, pg, dg, gategain_grad, skip_grad = lax.psum(
        (small_part[2 * state : 2 * state + heads], pg[:5], dg[:2, :heads], gategain_part, skip_part),
        every)
    return (
        block_output, input_grad, normgain_grad, zproj_grad, xproj_grad, bcproj_t.T, dtproj_t.T,
        pg[:4], pg[4], bg[:4], bg[4], dg[0], dg[1], skip_grad, gategain_grad, outproj_grad)


def solution(mesh):
    batch, tensor = mesh.shape["batch"], mesh.shape["tensor"]
    z = batch // 4
    split = Mesh(mesh.devices.reshape(z, 2, 2, tensor), ("z", "x", "core", "tensor"))
    rows = ("z", "x", "core")
    placed = (
        P(rows, "tensor", None), P(rows, None), P(), P(None, "tensor"), P(None, "tensor"), P(),
        P(None, "tensor"), P(None, "tensor"), P("tensor"), P(), P(), P("tensor"), P("tensor"),
        P("tensor"), P("tensor"), P("tensor", None), P(rows, "tensor", None))
    given = (
        P(rows, "tensor", None), P(rows, "tensor", None), P(), P(None, "tensor"), P(None, "tensor"),
        P(), P(None, "tensor"), P(None, "tensor"), P("tensor"), P(), P(), P("tensor"), P("tensor"),
        P("tensor"), P("tensor"), P("tensor", None))
    return jax.shard_map(
        functools.partial(shards, tensor), mesh=split, in_specs=placed, out_specs=given,
        check_vma=False)
```
